256 devices in a mesh: row: 8 (over z_lo, x), col: 32 (over y, z_hi, core).
Axes of the slice: x: 4, y: 4, z: 8 (z_hi: 4, z_lo: 2; z = z_hi * 2 + z_lo), core: 2. Of those that a mesh axis runs over, the one named last changes fastest.
Arguments:
- adjoint_field: float32 [3, 256, 256, 256], P(None, 'col', 'row'), may hold values from -6 to 6
- velocity: float32 [3, 256, 256, 256], P(None, 'col', 'row'), may hold values from -6 to 6
- saved_field: bfloat16 [2, 3, 256, 256, 256], P(None, None, 'col', 'row'), may hold values from -6 to 6
- gradient_in: float32 [3, 256, 256, 256], P(None, 'col', 'row'), may hold values from -6 to 6
Outputs:
- adjoint_out: float32 [3, 256, 256, 256], P(None, 'col', 'row')
- velocity_gradient: float32 [3, 256, 256, 256], P(None, 'col', 'row')
The draws below stay inside these ranges and needn't reach their ends.
All inputs are finite; a program needn't handle non-finite values.
Results may differ from the reference program's by a relative error of at most 0.0011.
Values sent between devices are 32-bit elements; how exact they have to be, the bound alone decides.
A program may use at most 128 MiB of HBM per device.

```python
import jax
import jax.numpy as jnp
from jax import lax

N = 256


def level_of(key, dims, shards, least, top_value):
    level = 1.0
    for position, blocks in shards:
        heights = jax.random.uniform(jax.random.fold_in(jax.random.fold_in(key, 6), position), (blocks,), jnp.float32, least / len(shards), top_value / len(shards))
        level = level * jnp.repeat(jnp.exp(heights), dims[position] // blocks).reshape((-1,) + (1,) * (len(dims) - 1 - position))
    return level


def scatter_about(stream_key, dims, width, reach, pieces=(), dtype=jnp.bfloat16):
    result = width * jax.random.normal(stream_key, dims, jnp.float32)
    if pieces:
        result = result * level_of(stream_key, dims, pieces, -0.22, 0.18)
    return jnp.clip(result, -reach, reach).astype(dtype)


def setup_inputs(seed: int = 0) -> dict:
    seeds = jax.random.split(jax.random.key(seed), 5)
    adjoint_field = scatter_about(seeds[0], (3, N, N, N), 1.0, 6.0, ((1, 32), (2, 8)), jnp.float32)
    velocity = scatter_about(seeds[1], (3, N, N, N), 1.0, 6.0, ((1, 32), (2, 8)), jnp.float32)
    saved_field = scatter_about(seeds[2], (2, 3, N, N, N), 1.0, 6.0, ((2, 32), (3, 8)))
    gradient_in = scatter_about(seeds[3], (3, N, N, N), 0.5, 6.0, ((1, 32), (2, 8)), jnp.float32)
    return {"adjoint_field": adjoint_field, "velocity": velocity, "saved_field": saved_field, "gradient_in": gradient_in}


TIME_STEP = 0.1
DIFFUSIVITY = 0.5


def wavenumbers():
    index = jnp.arange(N)
    signed = jnp.where(index < N // 2, index, index - N).astype(jnp.float32)
    laplace = (2.0 * jnp.pi / N) * signed
    return jnp.where(index == N // 2, jnp.zeros_like(laplace), laplace)


def cross(first, second):
    return jnp.stack([first[1] * second[2] - first[2] * second[1],
                      first[2] * second[0] - first[0] * second[2],
                      first[0] * second[1] - first[1] * second[0]])


def curl_hat(spectral, deriv):
    deriv_p = deriv[:, None, None]
    deriv_q = deriv[None, :, None]
    deriv_r = deriv[None, None, :]
    return 1j * jnp.stack([deriv_q * spectral[2] - deriv_r * spectral[1],
                           deriv_r * spectral[0] - deriv_p * spectral[2],
                           deriv_p * spectral[1] - deriv_q * spectral[0]])


def section(spectral, velocity, ksquare, deriv):
    curl_field = jnp.fft.ifftn(curl_hat(spectral, deriv), axes=(1, 2, 3), norm="ortho").real.astype(jnp.float32)
    rate = jnp.fft.fftn(cross(curl_field, velocity), axes=(1, 2, 3), norm="ortho") - DIFFUSIVITY * ksquare * spectral
    return curl_field, rate


def reference(adjoint_field, velocity, saved_field, gradient_in):
    deriv = wavenumbers()
    ksquare = deriv[:, None, None] ** 2 + deriv[None, :, None] ** 2 + deriv[None, None, :] ** 2
    start = jnp.fft.fftn(adjoint_field, axes=(1, 2, 3), norm="ortho")
    curl_first, rate_first = section(start, velocity, ksquare, deriv)
    middle = start + TIME_STEP * rate_first
    curl_second, rate_second = section(middle, velocity, ksquare, deriv)
    final = start + (0.5 * TIME_STEP) * (rate_first + rate_second)
    adjoint_out = jnp.fft.ifftn(final, axes=(1, 2, 3), norm="ortho").real.astype(jnp.float32)
    first_low = lax.optimization_barrier(curl_first.astype(jnp.bfloat16)).astype(jnp.float32)
    second_low = lax.optimization_barrier(curl_second.astype(jnp.bfloat16)).astype(jnp.float32)
    terms = cross(saved_field[0].astype(jnp.float32), first_low) + cross(saved_field[1].astype(jnp.float32), second_low)
    velocity_gradient = gradient_in + (0.5 * TIME_STEP) * terms
    return adjoint_out, velocity_gradient
```

```python
import functools
import math

import jax
import jax.numpy as jnp
import ml_dtypes
import numpy as np
from jax import lax
from jax.experimental import pallas as pl
from jax.experimental.pallas import tpu as pltpu
from jax.sharding import PartitionSpec as P

TIME_STEP = 0.1
DIFFUSIVITY = 0.5
MESH = pl.DeviceIdType.MESH
LANES = 128
HALVES = 2


def line_tables(length):
    index = np.arange(length)
    signed = np.where(index < length // 2, index, index - length).astype(np.float64)
    laplace = 2.0 * math.pi / length * signed
    laplace[length // 2] = 0.0
    angle = 2.0 * math.pi / length * (index[:, None] * index[None, :] % length)
    wave = np.exp(1j * angle) / math.sqrt(length)
    first = ((wave * (1j * laplace)) @ wave.conj().T).real
    second = ((wave * (-(laplace**2))) @ wave.conj().T).real
    return first, second


def two_parts(table):
    high = table.astype(np.float32).astype(ml_dtypes.bfloat16)
    low = (table - high.astype(np.float64)).astype(np.float32).astype(ml_dtypes.bfloat16)
    return high, low


def split_parts(values):
    high = values.astype(jnp.bfloat16)
    low = (values - high.astype(jnp.float32)).astype(jnp.bfloat16)
    return high, low


def wait_bytes(ref, sem):
    pltpu.make_async_copy(ref, ref, sem).wait()


def kernel(
    rows, cols,
    a0, vel, saved, grad, left, right,
    out, vgrad,
    a1, curl0, line_r, qbuf, pbuf, qres, pres, qback, pback, send_sem, recv_sem,
):
    row, col = lax.axis_index("row"), lax.axis_index("col")
    n_p, n_q = a0.shape[1], a0.shape[2]
    length = a0.shape[3]

    barrier = pltpu.get_barrier_semaphore()

    def greet_row(j, carry):
        pl.semaphore_signal(barrier, inc=1, device_id=(lax.rem(row + j, rows), col), device_id_type=MESH)
        return carry

    def greet_col(j, carry):
        pl.semaphore_signal(barrier, inc=1, device_id=(row, lax.rem(col + j, cols)), device_id_type=MESH)
        return carry

    lax.fori_loop(1, cols, greet_col, 0)
    lax.fori_loop(1, rows, greet_row, 0)
    pl.semaphore_wait(barrier, rows + cols - 2)

    def send_lines(field, sec, half):
        lanes = pl.ds(half * LANES, LANES)
        qs, qr = send_sem.at[0, sec, half], recv_sem.at[0, sec, half]
        ps, pr = send_sem.at[1, sec, half], recv_sem.at[1, sec, half]

        def to_col(j, carry):
            other = lax.rem(col + j, cols)
            pltpu.make_async_remote_copy(
                src_ref=field.at[:, :, other, lanes],
                dst_ref=pbuf.at[sec, half, :, pl.ds(pl.multiple_of(col * n_p, n_p), n_p), :],
                send_sem=ps, recv_sem=pr, device_id=(row, other), device_id_type=MESH,
            ).start()
            return carry

        def to_row(j, carry):
            other = lax.rem(row + j, rows)
            pltpu.make_async_remote_copy(
                src_ref=field.at[:, other, :, lanes],
                dst_ref=qbuf.at[sec, half, :, pl.ds(pl.multiple_of(row * n_q, n_q), n_q), :],
                send_sem=qs, recv_sem=qr, device_id=(other, col), device_id_type=MESH,
            ).start()
            return carry

        lax.fori_loop(1, cols, to_col, 0)
        lax.fori_loop(1, rows, to_row, 0)
        pltpu.make_async_copy(
            field.at[:, :, col, lanes],
            pbuf.at[sec, half, :, pl.ds(pl.multiple_of(col * n_p, n_p), n_p), :], pr,
        ).start()
        pltpu.make_async_copy(
            field.at[:, row, :, lanes],
            qbuf.at[sec, half, :, pl.ds(pl.multiple_of(row * n_q, n_q), n_q), :], qr,
        ).start()

    def apply_left(table_rows, lines):
        high, low = split_parts(lines)
        stacked = jnp.concatenate([high, low, high], axis=0)
        return jnp.dot(left[table_rows, :], stacked, preferred_element_type=jnp.float32)

    first_rows, second_rows = pl.ds(0, length), pl.ds(length, length)

    def back_col(sec, half, kind, parts):
        ss, rs = send_sem.at[kind, sec, half], recv_sem.at[kind, sec, half]

        def to_col(j, carry):
            other = lax.rem(col + j, cols)
            pltpu.make_async_remote_copy(
                src_ref=pres.at[sec, half, parts, pl.ds(pl.multiple_of(other * n_p, n_p), n_p), :],
                dst_ref=pback.at[sec, half, parts, :, col, :],
                send_sem=ss, recv_sem=rs, device_id=(row, other), device_id_type=MESH,
            ).start()
            return carry

        lax.fori_loop(1, cols, to_col, 0)
        pltpu.make_async_copy(
            pres.at[sec, half, parts, pl.ds(pl.multiple_of(col * n_p, n_p), n_p), :],
            pback.at[sec, half, parts, :, col, :], rs,
        ).start()

    def back_row(sec, half, kind, parts):
        ss, rs = send_sem.at[kind, sec, half], recv_sem.at[kind, sec, half]

        def to_row(j, carry):
            other = lax.rem(row + j, rows)
            pltpu.make_async_remote_copy(
                src_ref=qres.at[sec, half, parts, pl.ds(pl.multiple_of(other * n_q, n_q), n_q), :],
                dst_ref=qback.at[sec, half, parts, row],
                send_sem=ss, recv_sem=rs, device_id=(other, col), device_id_type=MESH,
            ).start()
            return carry

        lax.fori_loop(1, rows, to_row, 0)
        pltpu.make_async_copy(
            qres.at[sec, half, parts, pl.ds(pl.multiple_of(row * n_q, n_q), n_q), :],
            qback.at[sec, half, parts, row], rs,
        ).start()

    two, three = pl.ds(0, 2), pl.ds(2, 3)

    def line_ops(sec, half):
        wait_bytes(pbuf.at[sec, half], recv_sem.at[1, sec, half])
        for place, member in ((0, 1), (1, 2)):
            pres[sec, half, place] = apply_left(first_rows, pbuf[sec, half, member])
        back_col(sec, half, 3, two)
        wait_bytes(qbuf.at[sec, half], recv_sem.at[0, sec, half])
        for place, member in ((0, 0), (1, 2)):
            qres[sec, half, place] = apply_left(first_rows, qbuf[sec, half, member])
        back_row(sec, half, 2, two)
        for member in range(3):
            pres[sec, half, 2 + member] = apply_left(second_rows, pbuf[sec, half, member])
        back_col(sec, half, 5, three)
        for member in range(3):
            qres[sec, half, 2 + member] = apply_left(second_rows, qbuf[sec, half, member])
        back_row(sec, half, 4, three)

    def wait_back(sec, half):
        wait_bytes(qback.at[sec, half, two], recv_sem.at[2, sec, half])
        wait_bytes(pback.at[sec, half, two], recv_sem.at[3, sec, half])
        wait_bytes(qback.at[sec, half, three], recv_sem.at[4, sec, half])
        wait_bytes(pback.at[sec, half, three], recv_sem.at[5, sec, half])

    def along_r(field):
        def plane(p, carry):
            for member in range(3):
                high, low = split_parts(field[member, p])
                stacked = jnp.concatenate([high, low, high], axis=1)
                if member < 2:
                    both = jnp.dot(stacked, right[...], preferred_element_type=jnp.float32)
                    line_r[member, p] = both[:, :length]
                    line_r[2 + member, p] = both[:, length:]
                else:
                    line_r[4, p] = jnp.dot(stacked, right[:, length:], preferred_element_type=jnp.float32)
            return carry

        lax.fori_loop(0, n_p, plane, 0)

    def curl_at(sec, half, p, lanes):
        dq0, dq2 = qback[sec, half, 0, p], qback[sec, half, 1, p]
        dp1, dp2 = pback[sec, half, 0, p], pback[sec, half, 1, p]
        dr0, dr1 = line_r[0, p, :, lanes], line_r[1, p, :, lanes]
        return dq2 - dr1, dr0 - dp2, dp1 - dq0

    def laplace_at(sec, half, p, lanes, member):
        return line_r[2 + member, p, :, lanes] + qback[sec, half, 2 + member, p] + pback[sec, half, 2 + member, p]

    def cross(f, g):
        return (f[1] * g[2] - f[2] * g[1], f[2] * g[0] - f[0] * g[2], f[0] * g[1] - f[1] * g[0])

    for half in range(HALVES):
        send_lines(a0, 0, half)
    along_r(a0)
    for half in range(HALVES):
        line_ops(0, half)

    for half in range(HALVES):
        lanes = pl.ds(half * LANES, LANES)
        wait_back(0, half)

        def first_step(p, carry):
            curl = curl_at(0, half, p, lanes)
            rate = cross(curl, [vel[member, p, :, lanes] for member in range(3)])
            for member in range(3):
                curl0[member, p, :, lanes] = curl[member].astype(jnp.bfloat16)
                a1[member, p, :, lanes] = a0[member, p, :, lanes] + (
                    TIME_STEP * rate[member]
                    + TIME_STEP * DIFFUSIVITY * laplace_at(0, half, p, lanes, member)
                )
            return carry

        lax.fori_loop(0, n_p, first_step, 0)
        send_lines(a1, 1, half)

    along_r(a1)

    def first_gradient(p, carry):
        low = [curl0[member, p].astype(jnp.float32) for member in range(3)]
        terms = cross([saved[0, member, p].astype(jnp.float32) for member in range(3)], low)
        for member in range(3):
            vgrad[member, p] = grad[member, p] + 0.5 * TIME_STEP * terms[member]
        return carry

    lax.fori_loop(0, n_p, first_gradient, 0)
    for half in range(HALVES):
        line_ops(1, half)

    for half in range(HALVES):
        lanes = pl.ds(half * LANES, LANES)
        wait_back(1, half)

        def last_step(p, carry):
            curl = curl_at(1, half, p, lanes)
            rate = cross(curl, [vel[member, p, :, lanes] for member in range(3)])
            low = [curl[member].astype(jnp.bfloat16).astype(jnp.float32) for member in range(3)]
            terms = cross([saved[1, member, p, :, lanes].astype(jnp.float32) for member in range(3)], low)
            for member in range(3):
                out[member, p, :, lanes] = (
                    0.5 * (a0[member, p, :, lanes] + a1[member, p, :, lanes])
                    + 0.5 * TIME_STEP * rate[member]
                    + 0.5 * TIME_STEP * DIFFUSIVITY * laplace_at(1, half, p, lanes, member)
                )
                vgrad[member, p, :, lanes] += 0.5 * TIME_STEP * terms[member]
            return carry

        lax.fori_loop(0, n_p, last_step, 0)

    for sec in range(2):
        for half in range(HALVES):
            sent_q, sent_p = pl.ds(0, length - n_q), pl.ds(0, length - n_p)
            wait_bytes(qbuf.at[sec, half, :, sent_q], send_sem.at[0, sec, half])
            wait_bytes(pbuf.at[sec, half, :, sent_p], send_sem.at[1, sec, half])
            wait_bytes(qres.at[sec, half, two, sent_q], send_sem.at[2, sec, half])
            wait_bytes(pres.at[sec, half, two, sent_p], send_sem.at[3, sec, half])
            wait_bytes(qres.at[sec, half, three, sent_q], send_sem.at[4, sec, half])
            wait_bytes(pres.at[sec, half, three, sent_p], send_sem.at[5, sec, half])


def solution(mesh):
    rows, cols = mesh.shape["row"], mesh.shape["col"]

    def local(adjoint_field, velocity, saved_field, gradient_in):
        _, n_p, n_q, length = adjoint_field.shape
        first, second = line_tables(length)
        high, low = two_parts(np.concatenate([first, second], axis=0))
        left = jnp.asarray(np.concatenate([high, high, low], axis=1))
        high, low = two_parts(np.concatenate([first.T, second.T], axis=1))
        right = jnp.asarray(np.concatenate([high, high, low], axis=0))
        vmem = pl.BlockSpec(memory_space=pltpu.VMEM)
        field = jax.ShapeDtypeStruct(adjoint_field.shape, jnp.float32)
        lines = (2, HALVES, 3, length, LANES)
        results = (2, HALVES, 5, length, LANES)
        back = (2, HALVES, 5, n_p, n_q, LANES)
        return pl.pallas_call(
            functools.partial(kernel, rows, cols),
            out_shape=(field, field),
            in_specs=[vmem] * 6,
            out_specs=(vmem, vmem),
            scratch_shapes=[
                pltpu.VMEM(field.shape, jnp.float32),
                pltpu.VMEM(field.shape, jnp.bfloat16),
                pltpu.VMEM((5, n_p, n_q, length), jnp.float32),
                pltpu.VMEM(lines, jnp.float32),
                pltpu.VMEM(lines, jnp.float32),
                pltpu.VMEM(results, jnp.float32),
                pltpu.VMEM(results, jnp.float32),
                pltpu.VMEM(back, jnp.float32),
                pltpu.VMEM(back, jnp.float32),
                pltpu.SemaphoreType.DMA((6, 2, HALVES)),
                pltpu.SemaphoreType.DMA((6, 2, HALVES)),
            ],
            compiler_params=pltpu.CompilerParams(
                collective_id=0, has_side_effects=True, vmem_limit_bytes=48 * 2**20
            ),
        )(adjoint_field, velocity, saved_field, gradient_in, left, right)

    placed = P(None, "col", "row", None)
    return jax.shard_map(
        local,
        mesh=mesh,
        in_specs=(placed, placed, P(None, None, "col", "row", None), placed),
        out_specs=(placed, placed),
        check_vma=False,
    )
```

```python
import functools
import math

import jax
import jax.numpy as jnp
import ml_dtypes
import numpy as np
from jax import lax
from jax.experimental import pallas as pl
from jax.experimental.pallas import tpu as pltpu
from jax.sharding import PartitionSpec as P

TIME_STEP = 0.1
DIFFUSIVITY = 0.5
MESH = pl.DeviceIdType.MESH
LANES = 128
HALVES = 2


def line_tables(length):
    index = np.arange(length)
    signed = np.where(index < length // 2, index, index - length).astype(np.float64)
    laplace = 2.0 * math.pi / length * signed
    laplace[length // 2] = 0.0
    angle = 2.0 * math.pi / length * (index[:, None] * index[None, :] % length)
    wave = np.exp(1j * angle) / math.sqrt(length)
    first = ((wave * (1j * laplace)) @ wave.conj().T).real
    second = ((wave * (-(laplace**2))) @ wave.conj().T).real
    return first, second


def two_parts(table):
    high = table.astype(np.float32).astype(ml_dtypes.bfloat16)
    low = (table - high.astype(np.float64)).astype(np.float32).astype(ml_dtypes.bfloat16)
    return high, low


def split_parts(values):
    high = values.astype(jnp.bfloat16)
    low = (values - high.astype(jnp.float32)).astype(jnp.bfloat16)
    return high, low


def wait_bytes(ref, sem):
    pltpu.make_async_copy(ref, ref, sem).wait()


def kernel(
    rows, cols,
    a0, vel, saved, grad, left_p, left_q, right,
    out, vgrad,
    a1, mate, curl0, line_r, qbuf, pbuf, qres, pres, qback, pback, send_sem, recv_sem,
):
    row, col = lax.axis_index("row"), lax.axis_index("col")
    n_p, n_q, length = a0.shape[1], a0.shape[2], a0.shape[3]
    half_q = length // 2
    block_p = length // 4

    zl, x = lax.div(row, 4), lax.rem(row, 4)
    zh, spot = lax.rem(lax.div(col, 2), 4), lax.div(col, 8) * 2 + lax.rem(col, 2)
    mate_row = lax.rem(row + 4, rows)
    near = lax.rem(zh + 3 + 2 * zl, 4)
    far = lax.rem(zh + 2, 4)
    above, below = lax.rem(zh + 1, 4), lax.rem(zh + 3, 4)

    def col_of(spot_there, zh_there):
        return lax.div(spot_there, 2) * 8 + zh_there * 2 + lax.rem(spot_there, 2)

    def spot_at(j):
        return lax.rem(spot + j, 8)

    barrier = pltpu.get_barrier_semaphore()

    def greet(row_there, col_there):
        pl.semaphore_signal(barrier, inc=1, device_id=(row_there, col_there), device_id_type=MESH)

    def greet_spots(j, carry):
        there = spot_at(j)
        greet(row, col_of(there, above))
        greet(row, col_of(there, below))
        greet(mate_row, col_of(there, near))
        greet(mate_row, col_of(there, far))
        return carry

    def greet_zh(j, carry):
        greet(row, col_of(spot_at(j), zh))
        return carry

    def greet_x(j, carry):
        greet(zl * 4 + lax.rem(x + j, 4), col)
        return carry

    greet(mate_row, col)
    lax.fori_loop(0, 8, greet_spots, 0)
    lax.fori_loop(1, 8, greet_zh, 0)
    lax.fori_loop(1, 4, greet_x, 0)
    pl.semaphore_wait(barrier, 1 + 32 + 7 + 3)

    def remote(src, dst, kind, sec, half, row_there, col_there):
        pltpu.make_async_remote_copy(
            src_ref=src, dst_ref=dst, send_sem=send_sem.at[kind, sec, half], recv_sem=recv_sem.at[kind, sec, half],
            device_id=(row_there, col_there), device_id_type=MESH,
        ).start()

    def here(src, dst, kind, sec, half):
        pltpu.make_async_copy(src, dst, recv_sem.at[kind, sec, half]).start()

    def p_line(field, sec, half, row_there, spot_there, zh_there, role):
        lanes = pl.ds(half * LANES, LANES)
        line = col_of(spot_there, lax.rem(zh_there + 4 - role, 4))
        return (
            field.at[:, :, line, lanes],
            pbuf.at[sec, half, role, :, pl.ds(pl.multiple_of(col * n_p, n_p), n_p), :],
        )

    def send_p(field, sec, half, row_there, zh_there, first):
        def to_spot(j, carry):
            there = spot_at(j)
            for role in range(2):
                src, dst = p_line(field, sec, half, row_there, there, zh_there, role)
                remote(src, dst, 1, sec, half, row_there, col_of(there, zh_there))
            return carry

        lax.fori_loop(first, 8, to_spot, 0)

    def q_lines(field, half, sec, x_there, from_row):
        planes = pl.ds(x_there * 2, 2)
        return (
            field.at[:, planes, :, pl.ds(half * LANES, LANES)],
            qbuf.at[sec, half, :, :, pl.ds(pl.multiple_of(from_row * n_q, n_q), n_q), :],
        )

    def send_q(field, sec, half, from_row):
        def to_x(j, carry):
            x_there = lax.rem(x + j, 4)
            src, dst = q_lines(field, half, sec, x_there, from_row)
            remote(src, dst, 0, sec, half, zl * 4 + x_there, col)
            return carry

        lax.fori_loop(1, 4, to_x, 0)
        src, dst = q_lines(field, half, sec, x, from_row)
        here(src, dst, 0, sec, half)

    def send_own(field, sec, half):
        lanes = pl.ds(half * LANES, LANES)
        remote(field.at[:, :, :, lanes], mate.at[sec, :, :, :, lanes], 4, sec, half, mate_row, col)
        send_p(field, sec, half, row, near, 0)
        send_p(field, sec, half, row, zh, 1)
        for role in range(2):
            src, dst = p_line(field, sec, half, row, spot, zh, role)
            here(src, dst, 1, sec, half)
        send_q(field, sec, half, row)

    def send_mate(sec, half):
        lanes = pl.ds(half * LANES, LANES)
        wait_bytes(mate.at[sec, :, :, :, lanes], recv_sem.at[4, sec, half])
        send_p(mate.at[sec], sec, half, mate_row, far, 0)
        send_p(mate.at[sec], sec, half, mate_row, near, 0)
        send_q(mate.at[sec], sec, half, mate_row)

    def stack(lines):
        high, low = split_parts(lines)
        return jnp.concatenate([high, low, high], axis=0)

    def p_ops(sec, half):
        wait_bytes(pbuf.at[sec, half], recv_sem.at[1, sec, half])
        for role, beside in ((0, below), (1, above)):
            lines = jnp.concatenate([pbuf[sec, half, role, 1], pbuf[sec, half, role, 2]], axis=1)
            table = jnp.concatenate([left_p[zh], left_p[beside]], axis=0)
            both = jnp.dot(table, stack(lines), preferred_element_type=jnp.float32)
            table = jnp.concatenate([left_p[zh, block_p:], left_p[beside, block_p:]], axis=0)
            second = jnp.dot(table, stack(pbuf[sec, half, role, 0]), preferred_element_type=jnp.float32)
            for at in range(2):
                base = at * 2 * block_p
                for member in range(2):
                    lanes = slice(member * LANES, (member + 1) * LANES)
                    pres[sec, half, role, member, at] = both[base : base + block_p, lanes]
                    pres[sec, half, role, 3 + member, at] = both[base + block_p : base + 2 * block_p, lanes]
                pres[sec, half, role, 2, at] = second[at * block_p : (at + 1) * block_p]

        def result(role, at, there):
            line = col_of(spot, lax.rem(zh + 4 - role, 4))
            return (
                pres.at[sec, half, role, :, at, pl.ds(pl.multiple_of(there * n_p, n_p), n_p), :],
                pback.at[sec, half, :, :, line, :],
            )

        def to_spot(j, carry):
            there = spot_at(j)
            for role, beside in ((0, below), (1, above)):
                src, dst = result(role, 1, there)
                remote(src, dst, 3, sec, half, row, col_of(there, beside))
            return carry

        def to_zh(j, carry):
            there = spot_at(j)
            for role in range(2):
                src, dst = result(role, 0, there)
                remote(src, dst, 3, sec, half, row, col_of(there, zh))
            return carry

        lax.fori_loop(0, 8, to_spot, 0)
        lax.fori_loop(1, 8, to_zh, 0)
        for role in range(2):
            src, dst = result(role, 0, spot)
            here(src, dst, 3, sec, half)

    def q_ops(sec, half):
        wait_bytes(qbuf.at[sec, half], recv_sem.at[0, sec, half])
        for member in range(3):
            lines = stack(jnp.concatenate([qbuf[sec, half, member, 0], qbuf[sec, half, member, 1]], axis=1))
            if member == 1:
                second = jnp.dot(left_q[zl, half_q:], lines, preferred_element_type=jnp.float32)
            else:
                both = jnp.dot(left_q[zl], lines, preferred_element_type=jnp.float32)
                second = both[half_q:]
            for plane in range(2):
                lanes = slice(plane * LANES, (plane + 1) * LANES)
                if member != 1:
                    qres[sec, half, member // 2, plane] = both[:half_q, lanes]
                qres[sec, half, 2 + member, plane] = second[:, lanes]

        def result(x_there):
            return (
                qres.at[sec, half, :, :, pl.ds(pl.multiple_of(x_there * n_q, n_q), n_q), :],
                qback.at[sec, half, :, pl.ds(x * 2, 2)],
            )

        def to_x(j, carry):
            x_there = lax.rem(x + j, 4)
            src, dst = result(x_there)
            remote(src, dst, 2, sec, half, zl * 4 + x_there, col)
            return carry

        lax.fori_loop(1, 4, to_x, 0)
        src, dst = result(x)
        here(src, dst, 2, sec, half)

    def wait_back(sec, half):
        wait_bytes(qback.at[sec, half], recv_sem.at[2, sec, half])
        wait_bytes(pback.at[sec, half], recv_sem.at[3, sec, half])

    def along_r(field):
        def plane(p, carry):
            for member in range(3):
                high, low = split_parts(field[member, p])
                stacked = jnp.concatenate([high, low, high], axis=1)
                if member < 2:
                    both = jnp.dot(stacked, right[...], preferred_element_type=jnp.float32)
                    line_r[member, p] = both[:, :length]
                    line_r[2 + member, p] = both[:, length:]
                else:
                    line_r[4, p] = jnp.dot(stacked, right[:, length:], preferred_element_type=jnp.float32)
            return carry

        lax.fori_loop(0, n_p, plane, 0)

    def curl_at(sec, half, p, lanes):
        dq0, dq2 = qback[sec, half, 0, p], qback[sec, half, 1, p]
        dp1, dp2 = pback[sec, half, 0, p], pback[sec, half, 1, p]
        dr0, dr1 = line_r[0, p, :, lanes], line_r[1, p, :, lanes]
        return dq2 - dr1, dr0 - dp2, dp1 - dq0

    def laplace_at(sec, half, p, lanes, member):
        return line_r[2 + member, p, :, lanes] + qback[sec, half, 2 + member, p] + pback[sec, half, 2 + member, p]

    def cross(f, g):
        return (f[1] * g[2] - f[2] * g[1], f[2] * g[0] - f[0] * g[2], f[0] * g[1] - f[1] * g[0])

    for half in range(HALVES):
        send_own(a0, 0, half)
    send_mate(0, 0)
    along_r(a0)
    send_mate(0, 1)
    for half in range(HALVES):
        p_ops(0, half)
        q_ops(0, half)

    for half in range(HALVES):
        lanes = pl.ds(half * LANES, LANES)
        wait_back(0, half)

        def first_step(p, carry):
            curl = curl_at(0, half, p, lanes)
            rate = cross(curl, [vel[member, p, :, lanes] for member in range(3)])
            for member in range(3):
                curl0[member, p, :, lanes] = curl[member].astype(jnp.bfloat16)
                a1[member, p, :, lanes] = a0[member, p, :, lanes] + (
                    TIME_STEP * rate[member]
                    + TIME_STEP * DIFFUSIVITY * laplace_at(0, half, p, lanes, member)
                )
            return carry

        lax.fori_loop(0, n_p, first_step, 0)
        send_own(a1, 1, half)

    send_mate(1, 0)
    along_r(a1)
    send_mate(1, 1)

    def first_gradient(p, carry):
        low = [curl0[member, p].astype(jnp.float32) for member in range(3)]
        terms = cross([saved[0, member, p].astype(jnp.float32) for member in range(3)], low)
        for member in range(3):
            vgrad[member, p] = grad[member, p] + 0.5 * TIME_STEP * terms[member]
        return carry

    lax.fori_loop(0, n_p, first_gradient, 0)
    for half in range(HALVES):
        p_ops(1, half)
        q_ops(1, half)

    for half in range(HALVES):
        lanes = pl.ds(half * LANES, LANES)
        wait_back(1, half)

        def last_step(p, carry):
            curl = curl_at(1, half, p, lanes)
            rate = cross(curl, [vel[member, p, :, lanes] for member in range(3)])
            low = [curl[member].astype(jnp.bfloat16).astype(jnp.float32) for member in range(3)]
            terms = cross([saved[1, member, p, :, lanes].astype(jnp.float32) for member in range(3)], low)
            for member in range(3):
                out[member, p, :, lanes] = (
                    0.5 * (a0[member, p, :, lanes] + a1[member, p, :, lanes])
                    + 0.5 * TIME_STEP * rate[member]
                    + 0.5 * TIME_STEP * DIFFUSIVITY * laplace_at(1, half, p, lanes, member)
                )
                vgrad[member, p, :, lanes] += 0.5 * TIME_STEP * terms[member]
            return carry

        lax.fori_loop(0, n_p, last_step, 0)

    for sec in range(2):
        for half in range(HALVES):
            wait_bytes(qbuf.at[sec, half, :, :, pl.ds(0, 6 * n_q)], send_sem.at[0, sec, half])
            wait_bytes(pbuf.at[sec, half, :, :, pl.ds(0, length - n_p)], send_sem.at[1, sec, half])
            wait_bytes(qres.at[sec, half, :, :, pl.ds(0, 3 * n_q)], send_sem.at[2, sec, half])
            wait_bytes(pback.at[sec, half, :, :, pl.ds(0, n_q - 2)], send_sem.at[3, sec, half])
            wait_bytes(mate.at[sec, :, :, :, pl.ds(half * LANES, LANES)], send_sem.at[4, sec, half])


def solution(mesh):
    rows, cols = mesh.shape["row"], mesh.shape["col"]

    def local(adjoint_field, velocity, saved_field, gradient_in):
        _, n_p, n_q, length = adjoint_field.shape
        first, second = line_tables(length)
        by_zh = np.arange(length).reshape(4, 4, -1).transpose(1, 0, 2).reshape(4, -1)
        by_zl = np.arange(length).reshape(2, -1)

        def left_table(groups):
            both = np.concatenate([first[groups], second[groups]], axis=1)
            high, low = two_parts(both)
            return jnp.asarray(np.concatenate([high, high, low], axis=2))

        high, low = two_parts(np.concatenate([first.T, second.T], axis=1))
        right = jnp.asarray(np.concatenate([high, high, low], axis=0))
        vmem = pl.BlockSpec(memory_space=pltpu.VMEM)
        field = jax.ShapeDtypeStruct(adjoint_field.shape, jnp.float32)
        q_lines = (2, HALVES, 3, 2, length, LANES)
        p_lines = (2, HALVES, 2, 3, length, LANES)
        q_results = (2, HALVES, 5, 2, length // 2, LANES)
        p_results = (2, HALVES, 2, 5, 2, length // 4, LANES)
        back = (2, HALVES, 5, n_p, n_q, LANES)
        return pl.pallas_call(
            functools.partial(kernel, rows, cols),
            out_shape=(field, field),
            in_specs=[vmem] * 7,
            out_specs=(vmem, vmem),
            scratch_shapes=[
                pltpu.VMEM(field.shape, jnp.float32),
                pltpu.VMEM((2, *field.shape), jnp.float32),
                pltpu.VMEM(field.shape, jnp.bfloat16),
                pltpu.VMEM((5, n_p, n_q, length), jnp.float32),
                pltpu.VMEM(q_lines, jnp.float32),
                pltpu.VMEM(p_lines, jnp.float32),
                pltpu.VMEM(q_results, jnp.float32),
                pltpu.VMEM(p_results, jnp.float32),
                pltpu.VMEM(back, jnp.float32),
                pltpu.VMEM(back, jnp.float32),
                pltpu.SemaphoreType.DMA((5, 2, HALVES)),
                pltpu.SemaphoreType.DMA((5, 2, HALVES)),
            ],
            compiler_params=pltpu.CompilerParams(
                collective_id=0, has_side_effects=True, vmem_limit_bytes=48 * 2**20
            ),
        )(adjoint_field, velocity, saved_field, gradient_in, left_table(by_zh), left_table(by_zl), right)

    placed = P(None, "col", "row", None)
    return jax.shard_map(
        local,
        mesh=mesh,
        in_specs=(placed, placed, P(None, None, "col", "row", None), placed),
        out_specs=(placed, placed),
        check_vma=False,
    )
```

```python
import functools
import math

import jax
import jax.numpy as jnp
import ml_dtypes
import numpy as np
from jax import lax
from jax.experimental import pallas as pl
from jax.experimental.pallas import tpu as pltpu
from jax.sharding import PartitionSpec as P

TIME_STEP = 0.1
DIFFUSIVITY = 0.5
MESH = pl.DeviceIdType.MESH
LANES = 128
HALVES = 2


def line_tables(length):
    index = np.arange(length)
    signed = np.where(index < length // 2, index, index - length).astype(np.float64)
    laplace = 2.0 * math.pi / length * signed
    laplace[length // 2] = 0.0
    angle = 2.0 * math.pi / length * (index[:, None] * index[None, :] % length)
    wave = np.exp(1j * angle) / math.sqrt(length)
    first = ((wave * (1j * laplace)) @ wave.conj().T).real
    second = ((wave * (-(laplace**2))) @ wave.conj().T).real
    return first, second


def two_parts(table):
    high = table.astype(np.float32).astype(ml_dtypes.bfloat16)
    low = (table - high.astype(np.float64)).astype(np.float32).astype(ml_dtypes.bfloat16)
    return high, low


def split_parts(values):
    high = values.astype(jnp.bfloat16)
    low = (values - high.astype(jnp.float32)).astype(jnp.bfloat16)
    return high, low


def wait_bytes(ref, sem):
    pltpu.make_async_copy(ref, ref, sem).wait()


def kernel(
    rows, cols,
    a0, vel, saved, grad, left_p, left_q, right,
    out, vgrad,
    a1, mate, curl0, line_r, qbuf, pbuf, qres, pres, qback, pback, send_sem, recv_sem, mate_send, mate_recv,
):
    row, col = lax.axis_index("row"), lax.axis_index("col")
    n_p, n_q, length = a0.shape[1], a0.shape[2], a0.shape[3]
    half_q = length // 2
    block_p = length // 4

    zl, x = lax.div(row, 4), lax.rem(row, 4)
    zh, spot = lax.rem(lax.div(col, 2), 4), lax.div(col, 8) * 2 + lax.rem(col, 2)
    mate_row = lax.rem(row + 4, rows)
    near = lax.rem(zh + 3 + 2 * zl, 4)
    far = lax.rem(zh + 2, 4)
    above, below = lax.rem(zh + 1, 4), lax.rem(zh + 3, 4)

    def col_of(spot_there, zh_there):
        return lax.div(spot_there, 2) * 8 + zh_there * 2 + lax.rem(spot_there, 2)

    def spot_at(j):
        return lax.rem(spot + j, 8)

    barrier = pltpu.get_barrier_semaphore()

    def greet(row_there, col_there):
        pl.semaphore_signal(barrier, inc=1, device_id=(row_there, col_there), device_id_type=MESH)

    def greet_spots(j, carry):
        there = spot_at(j)
        greet(row, col_of(there, above))
        greet(row, col_of(there, below))
        greet(mate_row, col_of(there, near))
        greet(mate_row, col_of(there, far))
        return carry

    def greet_zh(j, carry):
        greet(row, col_of(spot_at(j), zh))
        return carry

    def greet_x(j, carry):
        greet(zl * 4 + lax.rem(x + j, 4), col)
        return carry

    greet(mate_row, col)
    lax.fori_loop(0, 8, greet_spots, 0)
    lax.fori_loop(1, 8, greet_zh, 0)
    lax.fori_loop(1, 4, greet_x, 0)
    pl.semaphore_wait(barrier, 1 + 32 + 7 + 3)

    def remote(src, dst, kind, sec, half, row_there, col_there):
        pltpu.make_async_remote_copy(
            src_ref=src, dst_ref=dst, send_sem=send_sem.at[kind, sec, half], recv_sem=recv_sem.at[kind, sec, half],
            device_id=(row_there, col_there), device_id_type=MESH,
        ).start()

    def here(src, dst, kind, sec, half):
        pltpu.make_async_copy(src, dst, recv_sem.at[kind, sec, half]).start()

    def p_line(field, sec, half, row_there, spot_there, zh_there, role):
        lanes = pl.ds(half * LANES, LANES)
        line = col_of(spot_there, lax.rem(zh_there + 4 - role, 4))
        return (
            field.at[:, :, line, lanes],
            pbuf.at[sec, half, role, :, pl.ds(pl.multiple_of(col * n_p, n_p), n_p), :],
        )

    def send_line(field, sec, half, row_there, spot_there, zh_there, role):
        src, dst = p_line(field, sec, half, row_there, spot_there, zh_there, role)
        remote(src, dst, 1, sec, half, row_there, col_of(spot_there, zh_there))

    def q_lines(field, half, sec, x_there, from_row):
        planes = pl.ds(x_there * 2, 2)
        return (
            field.at[:, planes, :, pl.ds(half * LANES, LANES)],
            qbuf.at[sec, half, :, :, pl.ds(pl.multiple_of(from_row * n_q, n_q), n_q), :],
        )

    def send_q(field, sec, half, from_row):
        def to_x(j, carry):
            x_there = lax.rem(x + j, 4)
            src, dst = q_lines(field, half, sec, x_there, from_row)
            remote(src, dst, 0, sec, half, zl * 4 + x_there, col)
            return carry

        lax.fori_loop(1, 4, to_x, 0)
        src, dst = q_lines(field, half, sec, x, from_row)
        here(src, dst, 0, sec, half)

    def mate_part(c):
        y_there = lax.rem(lax.div(spot, 2) + c, 4)
        return y_there, pl.ds(pl.multiple_of(y_there * 8, 8), 8)

    def start_mate(field, sec, half, c):
        lanes = pl.ds(half * LANES, LANES)
        _, part = mate_part(c)
        pltpu.make_async_remote_copy(
            src_ref=field.at[:, :, part, lanes], dst_ref=mate.at[sec, :, :, part, lanes],
            send_sem=mate_send.at[sec, half], recv_sem=mate_recv.at[sec, half, c],
            device_id=(mate_row, col), device_id_type=MESH,
        ).start()

    def pass_mate(sec, half, c):
        y_there, part = mate_part(c)
        wait_bytes(mate.at[sec, :, :, part, pl.ds(half * LANES, LANES)], mate_recv.at[sec, half, c])
        for core in range(2):
            there = y_there * 2 + core
            for role in range(2):
                send_line(mate.at[sec], sec, half, mate_row, there, far, role)
                send_line(mate.at[sec], sec, half, mate_row, there, near, role)

    def send_near(field, sec, half):
        def to_spot(j, carry):
            for role in range(2):
                send_line(field, sec, half, row, spot_at(j), near, role)
            return carry

        lax.fori_loop(0, 8, to_spot, 0)

    def send_zh(field, sec, half):
        def to_spot(j, carry):
            for role in range(2):
                send_line(field, sec, half, row, spot_at(j), zh, role)
            return carry

        lax.fori_loop(1, 8, to_spot, 0)
        for role in range(2):
            src, dst = p_line(field, sec, half, row, spot, zh, role)
            here(src, dst, 1, sec, half)

    def parts(step):
        def body(c, carry):
            step(c)
            return carry

        lax.fori_loop(0, 4, body, 0)

    def send_rest(field, sec):
        def first_half(c):
            pass_mate(sec, 0, c)
            start_mate(field, sec, 1, c)

        parts(first_half)
        send_near(field, sec, 0)
        send_q(mate.at[sec], sec, 0, mate_row)
        send_zh(field, sec, 1)
        send_q(field, sec, 1, row)
        parts(lambda c: pass_mate(sec, 1, c))
        send_near(field, sec, 1)
        send_q(mate.at[sec], sec, 1, mate_row)

    def send_first(field, sec):
        parts(lambda c: start_mate(field, sec, 0, c))
        send_zh(field, sec, 0)
        send_q(field, sec, 0, row)

    def stack(lines):
        high, low = split_parts(lines)
        return jnp.concatenate([high, low, high], axis=0)

    def p_ops(sec, half):
        wait_bytes(pbuf.at[sec, half], recv_sem.at[1, sec, half])
        for role, beside in ((0, below), (1, above)):
            lines = jnp.concatenate([pbuf[sec, half, role, 1], pbuf[sec, half, role, 2]], axis=1)
            table = jnp.concatenate([left_p[zh], left_p[beside]], axis=0)
            both = jnp.dot(table, stack(lines), preferred_element_type=jnp.float32)
            table = jnp.concatenate([left_p[zh, block_p:], left_p[beside, block_p:]], axis=0)
            second = jnp.dot(table, stack(pbuf[sec, half, role, 0]), preferred_element_type=jnp.float32)
            for at in range(2):
                base = at * 2 * block_p
                for member in range(2):
                    lanes = slice(member * LANES, (member + 1) * LANES)
                    pres[sec, half, role, member, at] = both[base : base + block_p, lanes]
                    pres[sec, half, role, 3 + member, at] = both[base + block_p : base + 2 * block_p, lanes]
                pres[sec, half, role, 2, at] = second[at * block_p : (at + 1) * block_p]

        def result(role, at, there):
            line = col_of(spot, lax.rem(zh + 4 - role, 4))
            return (
                pres.at[sec, half, role, :, at, pl.ds(pl.multiple_of(there * n_p, n_p), n_p), :],
                pback.at[sec, half, :, :, line, :],
            )

        def to_spot(j, carry):
            there = spot_at(j)
            for role, beside in ((0, below), (1, above)):
                src, dst = result(role, 1, there)
                remote(src, dst, 3, sec, half, row, col_of(there, beside))
            return carry

        def to_zh(j, carry):
            there = spot_at(j)
            for role in range(2):
                src, dst = result(role, 0, there)
                remote(src, dst, 3, sec, half, row, col_of(there, zh))
            return carry

        lax.fori_loop(0, 8, to_spot, 0)
        lax.fori_loop(1, 8, to_zh, 0)
        for role in range(2):
            src, dst = result(role, 0, spot)
            here(src, dst, 3, sec, half)

    def q_ops(sec, half):
        wait_bytes(qbuf.at[sec, half], recv_sem.at[0, sec, half])
        for member in range(3):
            lines = stack(jnp.concatenate([qbuf[sec, half, member, 0], qbuf[sec, half, member, 1]], axis=1))
            if member == 1:
                second = jnp.dot(left_q[zl, half_q:], lines, preferred_element_type=jnp.float32)
            else:
                both = jnp.dot(left_q[zl], lines, preferred_element_type=jnp.float32)
                second = both[half_q:]
            for plane in range(2):
                lanes = slice(plane * LANES, (plane + 1) * LANES)
                if member != 1:
                    qres[sec, half, member // 2, plane] = both[:half_q, lanes]
                qres[sec, half, 2 + member, plane] = second[:, lanes]

        def result(x_there):
            return (
                qres.at[sec, half, :, :, pl.ds(pl.multiple_of(x_there * n_q, n_q), n_q), :],
                qback.at[sec, half, :, pl.ds(x * 2, 2)],
            )

        def to_x(j, carry):
            x_there = lax.rem(x + j, 4)
            src, dst = result(x_there)
            remote(src, dst, 2, sec, half, zl * 4 + x_there, col)
            return carry

        lax.fori_loop(1, 4, to_x, 0)
        src, dst = result(x)
        here(src, dst, 2, sec, half)

    def wait_back(sec, half):
        wait_bytes(qback.at[sec, half], recv_sem.at[2, sec, half])
        wait_bytes(pback.at[sec, half], recv_sem.at[3, sec, half])

    def along_r(field):
        def plane(p, carry):
            for member in range(3):
                high, low = split_parts(field[member, p])
                stacked = jnp.concatenate([high, low, high], axis=1)
                if member < 2:
                    both = jnp.dot(stacked, right[...], preferred_element_type=jnp.float32)
                    line_r[member, p] = both[:, :length]
                    line_r[2 + member, p] = both[:, length:]
                else:
                    line_r[4, p] = jnp.dot(stacked, right[:, length:], preferred_element_type=jnp.float32)
            return carry

        lax.fori_loop(0, n_p, plane, 0)

    def curl_at(sec, half, p, lanes):
        dq0, dq2 = qback[sec, half, 0, p], qback[sec, half, 1, p]
        dp1, dp2 = pback[sec, half, 0, p], pback[sec, half, 1, p]
        dr0, dr1 = line_r[0, p, :, lanes], line_r[1, p, :, lanes]
        return dq2 - dr1, dr0 - dp2, dp1 - dq0

    def laplace_at(sec, half, p, lanes, member):
        return line_r[2 + member, p, :, lanes] + qback[sec, half, 2 + member, p] + pback[sec, half, 2 + member, p]

    def cross(f, g):
        return (f[1] * g[2] - f[2] * g[1], f[2] * g[0] - f[0] * g[2], f[0] * g[1] - f[1] * g[0])

    send_first(a0, 0)
    send_rest(a0, 0)
    along_r(a0)
    for half in range(HALVES):
        p_ops(0, half)
        q_ops(0, half)

    for half in range(HALVES):
        lanes = pl.ds(half * LANES, LANES)
        wait_back(0, half)

        def first_step(p, carry):
            curl = curl_at(0, half, p, lanes)
            rate = cross(curl, [vel[member, p, :, lanes] for member in range(3)])
            for member in range(3):
                curl0[member, p, :, lanes] = curl[member].astype(jnp.bfloat16)
                a1[member, p, :, lanes] = a0[member, p, :, lanes] + (
                    TIME_STEP * rate[member]
                    + TIME_STEP * DIFFUSIVITY * laplace_at(0, half, p, lanes, member)
                )
            return carry

        lax.fori_loop(0, n_p, first_step, 0)
        if half == 0:
            send_first(a1, 1)

    send_rest(a1, 1)
    along_r(a1)

    def first_gradient(p, carry):
        low = [curl0[member, p].astype(jnp.float32) for member in range(3)]
        terms = cross([saved[0, member, p].astype(jnp.float32) for member in range(3)], low)
        for member in range(3):
            vgrad[member, p] = grad[member, p] + 0.5 * TIME_STEP * terms[member]
        return carry

    lax.fori_loop(0, n_p, first_gradient, 0)
    for half in range(HALVES):
        p_ops(1, half)
        q_ops(1, half)

    for half in range(HALVES):
        lanes = pl.ds(half * LANES, LANES)
        wait_back(1, half)

        def last_step(p, carry):
            curl = curl_at(1, half, p, lanes)
            rate = cross(curl, [vel[member, p, :, lanes] for member in range(3)])
            low = [curl[member].astype(jnp.bfloat16).astype(jnp.float32) for member in range(3)]
            terms = cross([saved[1, member, p, :, lanes].astype(jnp.float32) for member in range(3)], low)
            for member in range(3):
                out[member, p, :, lanes] = (
                    0.5 * (a0[member, p, :, lanes] + a1[member, p, :, lanes])
                    + 0.5 * TIME_STEP * rate[member]
                    + 0.5 * TIME_STEP * DIFFUSIVITY * laplace_at(1, half, p, lanes, member)
                )
                vgrad[member, p, :, lanes] += 0.5 * TIME_STEP * terms[member]
            return carry

        lax.fori_loop(0, n_p, last_step, 0)

    for sec in range(2):
        for half in range(HALVES):
            wait_bytes(qbuf.at[sec, half, :, :, pl.ds(0, 6 * n_q)], send_sem.at[0, sec, half])
            wait_bytes(pbuf.at[sec, half, :, :, pl.ds(0, length - n_p)], send_sem.at[1, sec, half])
            wait_bytes(qres.at[sec, half, :, :, pl.ds(0, 3 * n_q)], send_sem.at[2, sec, half])
            wait_bytes(pback.at[sec, half, :, :, pl.ds(0, n_q - 2)], send_sem.at[3, sec, half])
            wait_bytes(mate.at[sec, :, :, :, pl.ds(half * LANES, LANES)], mate_send.at[sec, half])


def solution(mesh):
    rows, cols = mesh.shape["row"], mesh.shape["col"]

    def local(adjoint_field, velocity, saved_field, gradient_in):
        _, n_p, n_q, length = adjoint_field.shape
        first, second = line_tables(length)
        by_zh = np.arange(length).reshape(4, 4, -1).transpose(1, 0, 2).reshape(4, -1)
        by_zl = np.arange(length).reshape(2, -1)

        def left_table(groups):
            both = np.concatenate([first[groups], second[groups]], axis=1)
            high, low = two_parts(both)
            return jnp.asarray(np.concatenate([high, high, low], axis=2))

        high, low = two_parts(np.concatenate([first.T, second.T], axis=1))
        right = jnp.asarray(np.concatenate([high, high, low], axis=0))
        vmem = pl.BlockSpec(memory_space=pltpu.VMEM)
        field = jax.ShapeDtypeStruct(adjoint_field.shape, jnp.float32)
        q_lines = (2, HALVES, 3, 2, length, LANES)
        p_lines = (2, HALVES, 2, 3, length, LANES)
        q_results = (2, HALVES, 5, 2, length // 2, LANES)
        p_results = (2, HALVES, 2, 5, 2, length // 4, LANES)
        back = (2, HALVES, 5, n_p, n_q, LANES)
        return pl.pallas_call(
            functools.partial(kernel, rows, cols),
            out_shape=(field, field),
            in_specs=[vmem] * 7,
            out_specs=(vmem, vmem),
            scratch_shapes=[
                pltpu.VMEM(field.shape, jnp.float32),
                pltpu.VMEM((2, *field.shape), jnp.float32),
                pltpu.VMEM(field.shape, jnp.bfloat16),
                pltpu.VMEM((5, n_p, n_q, length), jnp.float32),
                pltpu.VMEM(q_lines, jnp.float32),
                pltpu.VMEM(p_lines, jnp.float32),
                pltpu.VMEM(q_results, jnp.float32),
                pltpu.VMEM(p_results, jnp.float32),
                pltpu.VMEM(back, jnp.float32),
                pltpu.VMEM(back, jnp.float32),
                pltpu.SemaphoreType.DMA((4, 2, HALVES)),
                pltpu.SemaphoreType.DMA((4, 2, HALVES)),
                pltpu.SemaphoreType.DMA((2, HALVES)),
                pltpu.SemaphoreType.DMA((2, HALVES, 4)),
            ],
            compiler_params=pltpu.CompilerParams(
                collective_id=0, has_side_effects=True, vmem_limit_bytes=48 * 2**20
            ),
        )(adjoint_field, velocity, saved_field, gradient_in, left_table(by_zh), left_table(by_zl), right)

    placed = P(None, "col", "row", None)
    return jax.shard_map(
        local,
        mesh=mesh,
        in_specs=(placed, placed, P(None, None, "col", "row", None), placed),
        out_specs=(placed, placed),
        check_vma=False,
    )
```

```python
import functools
import math

import jax
import jax.numpy as jnp
import numpy as np
from jax import lax
from jax.experimental import pallas as pl
from jax.experimental.pallas import tpu as pltpu
from jax.sharding import PartitionSpec as P

TIME_STEP = 0.1
DIFFUSIVITY = 0.5
MESH = pl.DeviceIdType.MESH
LANES = 128
HALVES = 2


def line_tables(length):
    index = np.arange(length)
    signed = np.where(index < length // 2, index, index - length).astype(np.float64)
    laplace = 2.0 * math.pi / length * signed
    laplace[length // 2] = 0.0
    angle = 2.0 * math.pi / length * (index[:, None] * index[None, :] % length)
    wave = np.exp(1j * angle) / math.sqrt(length)
    first = ((wave * (1j * laplace)) @ wave.conj().T).real
    second = ((wave * (-(laplace**2))) @ wave.conj().T).real
    return first, second


def split_parts(values):
    high = values.astype(jnp.bfloat16)
    low = (values - high.astype(jnp.float32)).astype(jnp.bfloat16)
    return high, low


def wait_bytes(ref, sem):
    pltpu.make_async_copy(ref, ref, sem).wait()


def kernel(
    rows, cols,
    a0_in, vel_in, saved_in, grad_in, left_p_in, left_q_in, right_in,
    out_there, vgrad_there,
    out, vgrad, out_sem, a0, vel, saved, grad, left_p_f32, left_q_f32, right_f32, load_sem, left_p, left_q, right,
    a1, mate, curl0, line_r, qbuf, pbuf, qres, pres, qback, pback, send_sem, recv_sem, mate_send, mate_recv,
):
    row, col = lax.axis_index("row"), lax.axis_index("col")
    n_p, n_q, length = a0.shape[1], a0.shape[2], a0.shape[3]
    half_q = length // 2
    block_p = length // 4

    zl, x = lax.div(row, 4), lax.rem(row, 4)
    zh, spot = lax.rem(lax.div(col, 2), 4), lax.div(col, 8) * 2 + lax.rem(col, 2)
    mate_row = lax.rem(row + 4, rows)
    near = lax.rem(zh + 3 + 2 * zl, 4)
    above, below = lax.rem(zh + 1, 4), lax.rem(zh + 3, 4)

    def col_of(spot_there, zh_there):
        return lax.div(spot_there, 2) * 8 + zh_there * 2 + lax.rem(spot_there, 2)

    def spot_at(j):
        return lax.rem(spot + j, 8)

    loads = (
        (left_p_in, left_p_f32), (left_q_in, left_q_f32), (right_in, right_f32),
        (vel_in, vel), (grad_in, grad), (saved_in, saved),
    )
    for half in range(HALVES):
        for member in range(3):
            part = (member, slice(None), slice(None), pl.ds(half * LANES, LANES))
            pltpu.make_async_copy(a0_in.at[part], a0.at[part], load_sem.at[half]).start()
    for at, (there, held) in enumerate(loads):
        pltpu.make_async_copy(there, held, load_sem.at[HALVES + at]).start()

    def loaded(first, last):
        for at in range(first, last):
            there, held = loads[at]
            pltpu.make_async_copy(there, held, load_sem.at[HALVES + at]).wait()

    barrier = pltpu.get_barrier_semaphore()

    def greet(row_there, col_there):
        pl.semaphore_signal(barrier, inc=1, device_id=(row_there, col_there), device_id_type=MESH)

    def greet_spots(j, carry):
        there = spot_at(j)
        greet(row, col_of(there, above))
        greet(row, col_of(there, below))
        greet(mate_row, col_of(there, near))
        return carry

    def greet_zh(j, carry):
        greet(row, col_of(spot_at(j), zh))
        return carry

    def greet_x(j, carry):
        greet(zl * 4 + lax.rem(x + j, 4), col)
        return carry

    greet(mate_row, col)
    lax.fori_loop(0, 8, greet_spots, 0)
    lax.fori_loop(1, 8, greet_zh, 0)
    lax.fori_loop(1, 4, greet_x, 0)
    pl.semaphore_wait(barrier, 1 + 24 + 7 + 3)

    def remote(src, dst, kind, sec, half, row_there, col_there):
        pltpu.make_async_remote_copy(
            src_ref=src, dst_ref=dst, send_sem=send_sem.at[kind, sec, half], recv_sem=recv_sem.at[kind, sec, half],
            device_id=(row_there, col_there), device_id_type=MESH,
        ).start()

    def here(src, dst, kind, sec, half):
        pltpu.make_async_copy(src, dst, recv_sem.at[kind, sec, half]).start()

    def p_line(field, sec, half, row_there, spot_there, zh_there, role):
        lanes = pl.ds(half * LANES, LANES)
        line = col_of(spot_there, lax.rem(zh_there + 4 - role, 4))
        return (
            field.at[:, :, line, lanes],
            pbuf.at[sec, half, role, :, lax.div(col, 8), zh, pl.ds(pl.multiple_of(lax.rem(col, 2) * n_p, n_p), n_p), :],
        )

    def send_line(field, sec, half, row_there, spot_there, zh_there, role, kind, arrival):
        src, dst = p_line(field, sec, half, row_there, spot_there, zh_there, role)
        pltpu.make_async_remote_copy(
            src_ref=src, dst_ref=dst, send_sem=send_sem.at[kind, sec, half], recv_sem=recv_sem.at[arrival, sec, half],
            device_id=(row_there, col_of(spot_there, zh_there)), device_id_type=MESH,
        ).start()

    near_arrival = (1 + 3 * zl, 5 - 4 * zl)

    def pass_on(sec, half):
        for role, source, there in ((0, below, above), (1, above, below)):
            lines = pbuf.at[sec, half, role, :, :, source]
            wait_bytes(lines, recv_sem.at[4 + role, sec, half])
            pltpu.make_async_remote_copy(
                src_ref=lines, dst_ref=pbuf.at[sec, half, 1 - role, :, :, source],
                send_sem=send_sem.at[5, sec, half], recv_sem=recv_sem.at[1, sec, half],
                device_id=(row, col_of(spot, there)), device_id_type=MESH,
            ).start()

    def q_lines(field, half, sec, x_there, from_row):
        planes = pl.ds(x_there * 2, 2)
        return (
            field.at[:, planes, :, pl.ds(half * LANES, LANES)],
            qbuf.at[sec, half, :, :, pl.ds(pl.multiple_of(from_row * n_q, n_q), n_q), :],
        )

    def send_q(field, sec, half, from_row):
        def to_x(j, carry):
            x_there = lax.rem(x + j, 4)
            src, dst = q_lines(field, half, sec, x_there, from_row)
            remote(src, dst, 0, sec, half, zl * 4 + x_there, col)
            return carry

        lax.fori_loop(1, 4, to_x, 0)
        src, dst = q_lines(field, half, sec, x, from_row)
        here(src, dst, 0, sec, half)

    def mate_part(c):
        y_there = lax.rem(lax.div(spot, 2) + c, 4)
        return y_there, pl.ds(pl.multiple_of(y_there * 8, 8), 8)

    def start_mate(field, sec, half, c):
        lanes = pl.ds(half * LANES, LANES)
        _, part = mate_part(c)
        pltpu.make_async_remote_copy(
            src_ref=field.at[:, :, part, lanes], dst_ref=mate.at[sec, :, :, part, lanes],
            send_sem=mate_send.at[sec, half], recv_sem=mate_recv.at[sec, half, c],
            device_id=(mate_row, col), device_id_type=MESH,
        ).start()

    def pass_mate(sec, half, c):
        y_there, part = mate_part(c)
        wait_bytes(mate.at[sec, :, :, part, pl.ds(half * LANES, LANES)], mate_recv.at[sec, half, c])
        for core in range(2):
            there = y_there * 2 + core
            for role in range(2):
                send_line(mate.at[sec], sec, half, mate_row, there, near, role, 4, near_arrival[role])

    def send_near(field, sec, half, c):
        y_there, _ = mate_part(c)
        for core in range(2):
            for role in range(2):
                send_line(field, sec, half, row, y_there * 2 + core, near, role, 4, near_arrival[role])

    def send_zh(field, sec, half):
        def to_spot(j, carry):
            for role in range(2):
                send_line(field, sec, half, row, spot_at(j), zh, role, 1, 1)
            return carry

        lax.fori_loop(1, 8, to_spot, 0)
        for role in range(2):
            src, dst = p_line(field, sec, half, row, spot, zh, role)
            here(src, dst, 1, sec, half)

    def parts(step):
        def body(c, carry):
            step(c)
            return carry

        lax.fori_loop(0, 4, body, 0)

    def first_sends(field, sec):
        parts(lambda c: (start_mate(field, sec, 0, c), send_near(field, sec, 0, c)))
        send_zh(field, sec, 0)
        send_q(field, sec, 0, row)

    def other_sends(field, sec):
        parts(lambda c: (pass_mate(sec, 0, c), start_mate(field, sec, 1, c)))
        parts(lambda c: send_near(field, sec, 1, c))
        send_zh(field, sec, 1)
        send_q(field, sec, 1, row)
        send_q(mate.at[sec], sec, 0, mate_row)
        parts(lambda c: pass_mate(sec, 1, c))
        pass_on(sec, 0)
        send_q(mate.at[sec], sec, 1, mate_row)
        pass_on(sec, 1)

    def line_ops(sec):
        for half in range(HALVES):
            p_ops(sec, half)
            q_ops(sec, half)

    def stack(lines):
        high, low = split_parts(lines)
        return jnp.concatenate([high, low, high], axis=0)

    def whole(lines):
        return lines.reshape(length, LANES)

    def p_ops(sec, half):
        wait_bytes(pbuf.at[sec, half, :, :, pl.ds(0, 3)], recv_sem.at[1, sec, half])
        for role, beside in ((0, below), (1, above)):
            lines = jnp.concatenate([whole(pbuf[sec, half, role, 1]), whole(pbuf[sec, half, role, 2])], axis=1)
            table = jnp.concatenate([left_p[zh], left_p[beside]], axis=0)
            both = jnp.dot(table, stack(lines), preferred_element_type=jnp.float32)
            table = jnp.concatenate([left_p[zh, block_p:], left_p[beside, block_p:]], axis=0)
            second = jnp.dot(table, stack(whole(pbuf[sec, half, role, 0])), preferred_element_type=jnp.float32)
            for at in range(2):
                base = at * 2 * block_p
                for member in range(2):
                    lanes = slice(member * LANES, (member + 1) * LANES)
                    pres[sec, half, role, member, at] = both[base : base + block_p, lanes]
                    pres[sec, half, role, 3 + member, at] = both[base + block_p : base + 2 * block_p, lanes]
                pres[sec, half, role, 2, at] = second[at * block_p : (at + 1) * block_p]

        def result(role, at, there):
            line = col_of(spot, lax.rem(zh + 4 - role, 4))
            return (
                pres.at[sec, half, role, :, at, pl.ds(pl.multiple_of(there * n_p, n_p), n_p), :],
                pback.at[sec, half, :, :, line, :],
            )

        def to_spot(j, carry):
            there = spot_at(j)
            for role, beside in ((0, below), (1, above)):
                src, dst = result(role, 1, there)
                remote(src, dst, 3, sec, half, row, col_of(there, beside))
            return carry

        def to_zh(j, carry):
            there = spot_at(j)
            for role in range(2):
                src, dst = result(role, 0, there)
                remote(src, dst, 3, sec, half, row, col_of(there, zh))
            return carry

        lax.fori_loop(0, 8, to_spot, 0)
        lax.fori_loop(1, 8, to_zh, 0)
        for role in range(2):
            src, dst = result(role, 0, spot)
            here(src, dst, 3, sec, half)

    def q_ops(sec, half):
        wait_bytes(qbuf.at[sec, half], recv_sem.at[0, sec, half])
        for member in range(3):
            lines = stack(jnp.concatenate([qbuf[sec, half, member, 0], qbuf[sec, half, member, 1]], axis=1))
            if member == 1:
                second = jnp.dot(left_q[zl, half_q:], lines, preferred_element_type=jnp.float32)
            else:
                both = jnp.dot(left_q[zl], lines, preferred_element_type=jnp.float32)
                second = both[half_q:]
            for plane in range(2):
                lanes = slice(plane * LANES, (plane + 1) * LANES)
                if member != 1:
                    qres[sec, half, member // 2, plane] = both[:half_q, lanes]
                qres[sec, half, 2 + member, plane] = second[:, lanes]

        def result(x_there):
            return (
                qres.at[sec, half, :, :, pl.ds(pl.multiple_of(x_there * n_q, n_q), n_q), :],
                qback.at[sec, half, :, pl.ds(x * 2, 2)],
            )

        def to_x(j, carry):
            x_there = lax.rem(x + j, 4)
            src, dst = result(x_there)
            remote(src, dst, 2, sec, half, zl * 4 + x_there, col)
            return carry

        lax.fori_loop(1, 4, to_x, 0)
        src, dst = result(x)
        here(src, dst, 2, sec, half)

    def wait_back(sec, half):
        wait_bytes(qback.at[sec, half], recv_sem.at[2, sec, half])
        wait_bytes(pback.at[sec, half], recv_sem.at[3, sec, half])

    def along_r(field):
        def plane(p, carry):
            for member in range(3):
                high, low = split_parts(field[member, p])
                stacked = jnp.concatenate([high, low, high], axis=1)
                if member < 2:
                    both = jnp.dot(stacked, right[...], preferred_element_type=jnp.float32)
                    line_r[member, p] = both[:, :length]
                    line_r[2 + member, p] = both[:, length:]
                else:
                    line_r[4, p] = jnp.dot(stacked, right[:, length:], preferred_element_type=jnp.float32)
            return carry

        lax.fori_loop(0, n_p, plane, 0)

    def curl_at(sec, half, p, lanes):
        dq0, dq2 = qback[sec, half, 0, p], qback[sec, half, 1, p]
        dp1, dp2 = pback[sec, half, 0, p], pback[sec, half, 1, p]
        dr0, dr1 = line_r[0, p, :, lanes], line_r[1, p, :, lanes]
        return dq2 - dr1, dr0 - dp2, dp1 - dq0

    def laplace_at(sec, half, p, lanes, member):
        return line_r[2 + member, p, :, lanes] + qback[sec, half, 2 + member, p] + pback[sec, half, 2 + member, p]

    def cross(f, g):
        return (f[1] * g[2] - f[2] * g[1], f[2] * g[0] - f[0] * g[2], f[0] * g[1] - f[1] * g[0])

    def first_gradient(p, carry):
        low = [curl0[member, p].astype(jnp.float32) for member in range(3)]
        terms = cross([saved[0, member, p].astype(jnp.float32) for member in range(3)], low)
        for member in range(3):
            vgrad[member, p] = grad[member, p] + 0.5 * TIME_STEP * terms[member]
        return carry

    for half in range(HALVES):
        wait_bytes(a0.at[:, :, :, pl.ds(half * LANES, LANES)], load_sem.at[half])
    first_sends(a0, 0)
    loaded(0, 3)
    for table, held, axis in ((left_p_f32, left_p, 2), (left_q_f32, left_q, 2), (right_f32, right, 0)):
        high, low = split_parts(table[...])
        held[...] = jnp.concatenate([high, high, low], axis=axis)
    other_sends(a0, 0)
    line_ops(0)
    along_r(a0)
    loaded(3, 6)

    for half in range(HALVES):
        lanes = pl.ds(half * LANES, LANES)
        wait_back(0, half)

        def first_step(p, carry):
            curl = curl_at(0, half, p, lanes)
            rate = cross(curl, [vel[member, p, :, lanes] for member in range(3)])
            for member in range(3):
                curl0[member, p, :, lanes] = curl[member].astype(jnp.bfloat16)
                a1[member, p, :, lanes] = a0[member, p, :, lanes] + (
                    TIME_STEP * rate[member]
                    + TIME_STEP * DIFFUSIVITY * laplace_at(0, half, p, lanes, member)
                )
            return carry

        lax.fori_loop(0, n_p, first_step, 0)
        if half == 0:
            first_sends(a1, 1)

    other_sends(a1, 1)
    line_ops(1)
    along_r(a1)
    lax.fori_loop(0, n_p, first_gradient, 0)

    for half in range(HALVES):
        lanes = pl.ds(half * LANES, LANES)
        wait_back(1, half)

        def last_step(p, carry):
            curl = curl_at(1, half, p, lanes)
            rate = cross(curl, [vel[member, p, :, lanes] for member in range(3)])
            low = [curl[member].astype(jnp.bfloat16).astype(jnp.float32) for member in range(3)]
            terms = cross([saved[1, member, p, :, lanes].astype(jnp.float32) for member in range(3)], low)
            for member in range(3):
                out[member, p, :, lanes] = (
                    0.5 * (a0[member, p, :, lanes] + a1[member, p, :, lanes])
                    + 0.5 * TIME_STEP * rate[member]
                    + 0.5 * TIME_STEP * DIFFUSIVITY * laplace_at(1, half, p, lanes, member)
                )
                vgrad[member, p, :, lanes] += 0.5 * TIME_STEP * terms[member]
            return carry

        lax.fori_loop(0, n_p, last_step, 0)
        for at, (held, there) in enumerate(((out, out_there), (vgrad, vgrad_there))):
            part = held.at[:, :, :, lanes]
            pltpu.make_async_copy(part, there.at[:, :, :, lanes], out_sem.at[at, half]).start()

    for sec in range(2):
        for half in range(HALVES):
            wait_bytes(qbuf.at[sec, half, :, :, pl.ds(0, 6 * n_q)], send_sem.at[0, sec, half])
            wait_bytes(pback.at[sec, half, pl.ds(0, 3), :, pl.ds(0, 14)], send_sem.at[1, sec, half])
            wait_bytes(pback.at[sec, half, pl.ds(0, 3)], send_sem.at[4, sec, half])
            wait_bytes(pback.at[sec, half, pl.ds(0, 3), :, pl.ds(0, 16)], send_sem.at[5, sec, half])
            wait_bytes(qres.at[sec, half, :, :, pl.ds(0, 3 * n_q)], send_sem.at[2, sec, half])
            wait_bytes(pback.at[sec, half, :, :, pl.ds(0, n_q - 2)], send_sem.at[3, sec, half])
            wait_bytes(mate.at[sec, :, :, :, pl.ds(half * LANES, LANES)], mate_send.at[sec, half])
            for at, held in enumerate((out, vgrad)):
                if sec == 0:
                    wait_bytes(held.at[:, :, :, pl.ds(half * LANES, LANES)], out_sem.at[at, half])


def solution(mesh):
    rows, cols = mesh.shape["row"], mesh.shape["col"]

    def local(adjoint_field, velocity, saved_field, gradient_in):
        _, n_p, n_q, length = adjoint_field.shape
        first, second = line_tables(length)
        by_zh = np.arange(length).reshape(4, 4, -1).transpose(1, 0, 2).reshape(4, -1)
        by_zl = np.arange(length).reshape(2, -1)

        def left_table(groups):
            return jnp.asarray(np.concatenate([first[groups], second[groups]], axis=1), jnp.float32)

        right = jnp.asarray(np.concatenate([first.T, second.T], axis=1), jnp.float32)
        field = jax.ShapeDtypeStruct(adjoint_field.shape, jnp.float32)
        q_lines = (2, HALVES, 3, 2, length, LANES)
        p_lines = (2, HALVES, 2, 3, 4, 4, length // 16, LANES)
        q_results = (2, HALVES, 5, 2, length // 2, LANES)
        p_results = (2, HALVES, 2, 5, 2, length // 4, LANES)
        back = (2, HALVES, 5, n_p, n_q, LANES)
        arrays = (
            adjoint_field, velocity, saved_field, gradient_in, left_table(by_zh), left_table(by_zl), right,
        )
        return pl.pallas_call(
            functools.partial(kernel, rows, cols),
            out_shape=(field, field),
            in_specs=[pl.BlockSpec(memory_space=pl.ANY)] * 7,
            out_specs=(pl.BlockSpec(memory_space=pl.ANY),) * 2,
            scratch_shapes=[
                pltpu.VMEM(field.shape, jnp.float32),
                pltpu.VMEM(field.shape, jnp.float32),
                pltpu.SemaphoreType.DMA((2, HALVES)),
                *(pltpu.VMEM(given.shape, given.dtype) for given in arrays),
                pltpu.SemaphoreType.DMA((HALVES + len(arrays) - 1,)),
                pltpu.VMEM((4, length // 2, 3 * length), jnp.bfloat16),
                pltpu.VMEM((2, length, 3 * length), jnp.bfloat16),
                pltpu.VMEM((3 * length, 2 * length), jnp.bfloat16),
                pltpu.VMEM(field.shape, jnp.float32),
                pltpu.VMEM((2, *field.shape), jnp.float32),
                pltpu.VMEM(field.shape, jnp.bfloat16),
                pltpu.VMEM((5, n_p, n_q, length), jnp.float32),
                pltpu.VMEM(q_lines, jnp.float32),
                pltpu.VMEM(p_lines, jnp.float32),
                pltpu.VMEM(q_results, jnp.float32),
                pltpu.VMEM(p_results, jnp.float32),
                pltpu.VMEM(back, jnp.float32),
                pltpu.VMEM(back, jnp.float32),
                pltpu.SemaphoreType.DMA((6, 2, HALVES)),
                pltpu.SemaphoreType.DMA((6, 2, HALVES)),
                pltpu.SemaphoreType.DMA((2, HALVES)),
                pltpu.SemaphoreType.DMA((2, HALVES, 4)),
            ],
            compiler_params=pltpu.CompilerParams(
                collective_id=0, has_side_effects=True, vmem_limit_bytes=60 * 2**20
            ),
        )(*arrays)

    placed = P(None, "col", "row", None)
    return jax.shard_map(
        local,
        mesh=mesh,
        in_specs=(placed, placed, P(None, None, "col", "row", None), placed),
        out_specs=(placed, placed),
        check_vma=False,
    )
```

```python
import functools
import math

import jax
import jax.numpy as jnp
import numpy as np
from jax import lax
from jax.experimental import pallas as pl
from jax.experimental.pallas import tpu as pltpu
from jax.sharding import PartitionSpec as P

TIME_STEP = 0.1
DIFFUSIVITY = 0.5
MESH = pl.DeviceIdType.MESH
LANES = 128
HALVES = 2


def line_tables(length):
    index = np.arange(length)
    signed = np.where(index < length // 2, index, index - length).astype(np.float64)
    laplace = 2.0 * math.pi / length * signed
    laplace[length // 2] = 0.0
    angle = 2.0 * math.pi / length * (index[:, None] * index[None, :] % length)
    wave = np.exp(1j * angle) / math.sqrt(length)
    first = ((wave * (1j * laplace)) @ wave.conj().T).real
    second = ((wave * (-(laplace**2))) @ wave.conj().T).real
    return first, second


def split_parts(values):
    high = values.astype(jnp.bfloat16)
    low = (values - high.astype(jnp.float32)).astype(jnp.bfloat16)
    return high, low


def wait_bytes(ref, sem):
    pltpu.make_async_copy(ref, ref, sem).wait()


def kernel(
    rows, cols,
    a0_in, vel_in, saved_in, grad_in, left_p_in, left_q_in, right_in,
    out_there, vgrad_there,
    out, vgrad, out_sem, a0, vel, saved, grad, left_p_f32, left_q_f32, right_f32, load_sem, left_p, left_q, right,
    a1, mate, curl0, line_r, qbuf, pbuf, qres, pres, qback, pback, send_sem, recv_sem, p_recv, mate_send, mate_recv,
):
    row, col = lax.axis_index("row"), lax.axis_index("col")
    n_p, n_q, length = a0.shape[1], a0.shape[2], a0.shape[3]
    half_q = length // 2
    block_p = length // 4

    zl, x = lax.div(row, 4), lax.rem(row, 4)
    zh, spot = lax.rem(lax.div(col, 2), 4), lax.div(col, 8) * 2 + lax.rem(col, 2)
    mate_row = lax.rem(row + 4, rows)
    near = lax.rem(zh + 3 + 2 * zl, 4)
    above, below = lax.rem(zh + 1, 4), lax.rem(zh + 3, 4)

    def col_of(spot_there, zh_there):
        return lax.div(spot_there, 2) * 8 + zh_there * 2 + lax.rem(spot_there, 2)

    def spot_at(j):
        return lax.rem(spot + j, 8)

    loads = (
        (left_p_in, left_p_f32), (left_q_in, left_q_f32), (right_in, right_f32),
        (vel_in, vel), (grad_in, grad), (saved_in, saved),
    )
    for half in range(HALVES):
        for member in range(3):
            part = (member, slice(None), slice(None), pl.ds(half * LANES, LANES))
            pltpu.make_async_copy(a0_in.at[part], a0.at[part], load_sem.at[half]).start()
    for at, (there, held) in enumerate(loads):
        pltpu.make_async_copy(there, held, load_sem.at[HALVES + at]).start()

    def loaded(first, last):
        for at in range(first, last):
            there, held = loads[at]
            pltpu.make_async_copy(there, held, load_sem.at[HALVES + at]).wait()

    barrier = pltpu.get_barrier_semaphore()

    def greet(row_there, col_there):
        pl.semaphore_signal(barrier, inc=1, device_id=(row_there, col_there), device_id_type=MESH)

    def greet_spots(j, carry):
        there = spot_at(j)
        greet(row, col_of(there, above))
        greet(row, col_of(there, below))
        greet(mate_row, col_of(there, near))
        return carry

    def greet_zh(j, carry):
        greet(row, col_of(spot_at(j), zh))
        return carry

    def greet_x(j, carry):
        greet(zl * 4 + lax.rem(x + j, 4), col)
        return carry

    greet(mate_row, col)
    lax.fori_loop(0, 8, greet_spots, 0)
    lax.fori_loop(1, 8, greet_zh, 0)
    lax.fori_loop(1, 4, greet_x, 0)
    pl.semaphore_wait(barrier, 1 + 24 + 7 + 3)

    def remote(src, dst, kind, sec, half, row_there, col_there):
        pltpu.make_async_remote_copy(
            src_ref=src, dst_ref=dst, send_sem=send_sem.at[kind, sec, half], recv_sem=recv_sem.at[kind, sec, half],
            device_id=(row_there, col_there), device_id_type=MESH,
        ).start()

    def here(src, dst, kind, sec, half):
        pltpu.make_async_copy(src, dst, recv_sem.at[kind, sec, half]).start()

    def p_line(field, sec, half, row_there, spot_there, zh_there, role):
        lanes = pl.ds(half * LANES, LANES)
        line = col_of(spot_there, lax.rem(zh_there + 4 - role, 4))
        return (
            field.at[:, :, line, lanes],
            pbuf.at[sec, half, role, :, lax.div(col, 8), zh, pl.ds(pl.multiple_of(lax.rem(col, 2) * n_p, n_p), n_p), :],
        )

    def near_arrival(role, c):
        return (1 - zl) * (5 + c) if role else zl * (1 + c)

    def send_line(field, sec, half, row_there, spot_there, zh_there, role, kind, arrival):
        src, dst = p_line(field, sec, half, row_there, spot_there, zh_there, role)
        pltpu.make_async_remote_copy(
            src_ref=src, dst_ref=dst, send_sem=send_sem.at[kind, sec, half], recv_sem=p_recv.at[sec, half, arrival],
            device_id=(row_there, col_of(spot_there, zh_there)), device_id_type=MESH,
        ).start()

    def pass_on(sec, half, c):
        y_from = lax.rem(lax.div(spot, 2) + 4 - c, 4)
        for role, source, there in ((0, below, above), (1, above, below)):
            lines = pbuf.at[sec, half, role, :, y_from, source]
            wait_bytes(lines, p_recv.at[sec, half, 1 + 4 * role + c])
            pltpu.make_async_remote_copy(
                src_ref=lines, dst_ref=pbuf.at[sec, half, 1 - role, :, y_from, source],
                send_sem=send_sem.at[5, sec, half], recv_sem=p_recv.at[sec, half, 0],
                device_id=(row, col_of(spot, there)), device_id_type=MESH,
            ).start()

    def q_lines(field, half, sec, x_there, from_row):
        planes = pl.ds(x_there * 2, 2)
        return (
            field.at[:, planes, :, pl.ds(half * LANES, LANES)],
            qbuf.at[sec, half, :, :, pl.ds(pl.multiple_of(from_row * n_q, n_q), n_q), :],
        )

    def send_q(field, sec, half, from_row):
        def to_x(j, carry):
            x_there = lax.rem(x + j, 4)
            src, dst = q_lines(field, half, sec, x_there, from_row)
            remote(src, dst, 0, sec, half, zl * 4 + x_there, col)
            return carry

        lax.fori_loop(1, 4, to_x, 0)
        src, dst = q_lines(field, half, sec, x, from_row)
        here(src, dst, 0, sec, half)

    def mate_part(c):
        y_there = lax.rem(lax.div(spot, 2) + c, 4)
        return y_there, pl.ds(pl.multiple_of(y_there * 8, 8), 8)

    def start_mate(field, sec, half, c):
        lanes = pl.ds(half * LANES, LANES)
        _, part = mate_part(c)
        pltpu.make_async_remote_copy(
            src_ref=field.at[:, :, part, lanes], dst_ref=mate.at[sec, :, :, part, lanes],
            send_sem=mate_send.at[sec, half], recv_sem=mate_recv.at[sec, half, c],
            device_id=(mate_row, col), device_id_type=MESH,
        ).start()

    def pass_mate(sec, half, c):
        y_there, part = mate_part(c)
        wait_bytes(mate.at[sec, :, :, part, pl.ds(half * LANES, LANES)], mate_recv.at[sec, half, c])
        for core in range(2):
            there = y_there * 2 + core
            for role in range(2):
                send_line(mate.at[sec], sec, half, mate_row, there, near, role, 4, near_arrival(role, c))

    def send_near(field, sec, half, c):
        y_there, _ = mate_part(c)
        for core in range(2):
            for role in range(2):
                send_line(field, sec, half, row, y_there * 2 + core, near, role, 4, near_arrival(role, c))

    def send_zh(field, sec, half):
        def to_spot(j, carry):
            for role in range(2):
                send_line(field, sec, half, row, spot_at(j), zh, role, 1, 0)
            return carry

        lax.fori_loop(1, 8, to_spot, 0)
        for role in range(2):
            src, dst = p_line(field, sec, half, row, spot, zh, role)
            pltpu.make_async_copy(src, dst, p_recv.at[sec, half, 0]).start()

    def parts(step):
        def body(c, carry):
            step(c)
            return carry

        lax.fori_loop(0, 4, body, 0)

    def first_sends(field, sec):
        parts(lambda c: (start_mate(field, sec, 0, c), send_near(field, sec, 0, c)))
        send_zh(field, sec, 0)
        send_q(field, sec, 0, row)

    def other_sends(field, sec):
        parts(lambda c: (pass_mate(sec, 0, c), start_mate(field, sec, 1, c)))
        parts(lambda c: send_near(field, sec, 1, c))
        send_zh(field, sec, 1)
        send_q(field, sec, 1, row)
        send_q(mate.at[sec], sec, 0, mate_row)
        parts(lambda c: (pass_mate(sec, 1, c), pass_on(sec, 0, c)))
        send_q(mate.at[sec], sec, 1, mate_row)

    def line_ops(sec):
        q_ops(sec, 0)
        parts(lambda c: pass_on(sec, 1, c))
        p_ops(sec, 0)
        p_ops(sec, 1)
        q_ops(sec, 1)

    def stack(lines):
        high, low = split_parts(lines)
        return jnp.concatenate([high, low, high], axis=0)

    def whole(lines):
        return lines.reshape(length, LANES)

    def p_ops(sec, half):
        wait_bytes(pbuf.at[sec, half, :, :, pl.ds(0, 3)], p_recv.at[sec, half, 0])
        for role, beside in ((0, below), (1, above)):
            lines = jnp.concatenate([whole(pbuf[sec, half, role, 1]), whole(pbuf[sec, half, role, 2])], axis=1)
            table = jnp.concatenate([left_p[zh], left_p[beside]], axis=0)
            both = jnp.dot(table, stack(lines), preferred_element_type=jnp.float32)
            table = jnp.concatenate([left_p[zh, block_p:], left_p[beside, block_p:]], axis=0)
            second = jnp.dot(table, stack(whole(pbuf[sec, half, role, 0])), preferred_element_type=jnp.float32)
            for at in range(2):
                base = at * 2 * block_p
                for member in range(2):
                    lanes = slice(member * LANES, (member + 1) * LANES)
                    pres[sec, half, role, member, at] = both[base : base + block_p, lanes]
                    pres[sec, half, role, 3 + member, at] = both[base + block_p : base + 2 * block_p, lanes]
                pres[sec, half, role, 2, at] = second[at * block_p : (at + 1) * block_p]

        def result(role, at, there):
            line = col_of(spot, lax.rem(zh + 4 - role, 4))
            return (
                pres.at[sec, half, role, :, at, pl.ds(pl.multiple_of(there * n_p, n_p), n_p), :],
                pback.at[sec, half, :, :, line, :],
            )

        def to_spot(j, carry):
            there = spot_at(j)
            for role, beside in ((0, below), (1, above)):
                src, dst = result(role, 1, there)
                remote(src, dst, 3, sec, half, row, col_of(there, beside))
            return carry

        def to_zh(j, carry):
            there = spot_at(j)
            for role in range(2):
                src, dst = result(role, 0, there)
                remote(src, dst, 3, sec, half, row, col_of(there, zh))
            return carry

        lax.fori_loop(0, 8, to_spot, 0)
        lax.fori_loop(1, 8, to_zh, 0)
        for role in range(2):
            src, dst = result(role, 0, spot)
            here(src, dst, 3, sec, half)

    def q_ops(sec, half):
        wait_bytes(qbuf.at[sec, half], recv_sem.at[0, sec, half])
        for member in range(3):
            lines = stack(jnp.concatenate([qbuf[sec, half, member, 0], qbuf[sec, half, member, 1]], axis=1))
            if member == 1:
                second = jnp.dot(left_q[zl, half_q:], lines, preferred_element_type=jnp.float32)
            else:
                both = jnp.dot(left_q[zl], lines, preferred_element_type=jnp.float32)
                second = both[half_q:]
            for plane in range(2):
                lanes = slice(plane * LANES, (plane + 1) * LANES)
                if member != 1:
                    qres[sec, half, member // 2, plane] = both[:half_q, lanes]
                qres[sec, half, 2 + member, plane] = second[:, lanes]

        def result(x_there):
            return (
                qres.at[sec, half, :, :, pl.ds(pl.multiple_of(x_there * n_q, n_q), n_q), :],
                qback.at[sec, half, :, pl.ds(x * 2, 2)],
            )

        def to_x(j, carry):
            x_there = lax.rem(x + j, 4)
            src, dst = result(x_there)
            remote(src, dst, 2, sec, half, zl * 4 + x_there, col)
            return carry

        lax.fori_loop(1, 4, to_x, 0)
        src, dst = result(x)
        here(src, dst, 2, sec, half)

    def wait_back(sec, half):
        wait_bytes(qback.at[sec, half], recv_sem.at[2, sec, half])
        wait_bytes(pback.at[sec, half], recv_sem.at[3, sec, half])

    def along_r(field):
        def plane(p, carry):
            for member in range(3):
                high, low = split_parts(field[member, p])
                stacked = jnp.concatenate([high, low, high], axis=1)
                if member < 2:
                    both = jnp.dot(stacked, right[...], preferred_element_type=jnp.float32)
                    line_r[member, p] = both[:, :length]
                    line_r[2 + member, p] = both[:, length:]
                else:
                    line_r[4, p] = jnp.dot(stacked, right[:, length:], preferred_element_type=jnp.float32)
            return carry

        lax.fori_loop(0, n_p, plane, 0)

    def curl_at(sec, half, p, lanes):
        dq0, dq2 = qback[sec, half, 0, p], qback[sec, half, 1, p]
        dp1, dp2 = pback[sec, half, 0, p], pback[sec, half, 1, p]
        dr0, dr1 = line_r[0, p, :, lanes], line_r[1, p, :, lanes]
        return dq2 - dr1, dr0 - dp2, dp1 - dq0

    def laplace_at(sec, half, p, lanes, member):
        return line_r[2 + member, p, :, lanes] + qback[sec, half, 2 + member, p] + pback[sec, half, 2 + member, p]

    def cross(f, g):
        return (f[1] * g[2] - f[2] * g[1], f[2] * g[0] - f[0] * g[2], f[0] * g[1] - f[1] * g[0])

    def first_gradient(p, carry):
        low = [curl0[member, p].astype(jnp.float32) for member in range(3)]
        terms = cross([saved[0, member, p].astype(jnp.float32) for member in range(3)], low)
        for member in range(3):
            vgrad[member, p] = grad[member, p] + 0.5 * TIME_STEP * terms[member]
        return carry

    for half in range(HALVES):
        wait_bytes(a0.at[:, :, :, pl.ds(half * LANES, LANES)], load_sem.at[half])
    first_sends(a0, 0)
    loaded(0, 3)
    for table, held, axis in ((left_p_f32, left_p, 2), (left_q_f32, left_q, 2), (right_f32, right, 0)):
        high, low = split_parts(table[...])
        held[...] = jnp.concatenate([high, high, low], axis=axis)
    other_sends(a0, 0)
    line_ops(0)
    along_r(a0)
    loaded(3, 6)

    for half in range(HALVES):
        lanes = pl.ds(half * LANES, LANES)
        wait_back(0, half)

        def first_step(p, carry):
            curl = curl_at(0, half, p, lanes)
            rate = cross(curl, [vel[member, p, :, lanes] for member in range(3)])
            for member in range(3):
                curl0[member, p, :, lanes] = curl[member].astype(jnp.bfloat16)
                a1[member, p, :, lanes] = a0[member, p, :, lanes] + (
                    TIME_STEP * rate[member]
                    + TIME_STEP * DIFFUSIVITY * laplace_at(0, half, p, lanes, member)
                )
            return carry

        lax.fori_loop(0, n_p, first_step, 0)
        if half == 0:
            first_sends(a1, 1)

    other_sends(a1, 1)
    line_ops(1)
    along_r(a1)
    lax.fori_loop(0, n_p, first_gradient, 0)

    for half in range(HALVES):
        lanes = pl.ds(half * LANES, LANES)
        wait_back(1, half)

        def last_step(p, carry):
            curl = curl_at(1, half, p, lanes)
            rate = cross(curl, [vel[member, p, :, lanes] for member in range(3)])
            low = [curl[member].astype(jnp.bfloat16).astype(jnp.float32) for member in range(3)]
            terms = cross([saved[1, member, p, :, lanes].astype(jnp.float32) for member in range(3)], low)
            for member in range(3):
                out[member, p, :, lanes] = (
                    0.5 * (a0[member, p, :, lanes] + a1[member, p, :, lanes])
                    + 0.5 * TIME_STEP * rate[member]
                    + 0.5 * TIME_STEP * DIFFUSIVITY * laplace_at(1, half, p, lanes, member)
                )
                vgrad[member, p, :, lanes] += 0.5 * TIME_STEP * terms[member]
            return carry

        lax.fori_loop(0, n_p, last_step, 0)
        for at, (held, there) in enumerate(((out, out_there), (vgrad, vgrad_there))):
            part = held.at[:, :, :, lanes]
            pltpu.make_async_copy(part, there.at[:, :, :, lanes], out_sem.at[at, half]).start()

    for sec in range(2):
        for half in range(HALVES):
            wait_bytes(qbuf.at[sec, half, :, :, pl.ds(0, 6 * n_q)], send_sem.at[0, sec, half])
            wait_bytes(pback.at[sec, half, pl.ds(0, 3), :, pl.ds(0, 14)], send_sem.at[1, sec, half])
            wait_bytes(pback.at[sec, half, pl.ds(0, 3)], send_sem.at[4, sec, half])
            wait_bytes(pback.at[sec, half, pl.ds(0, 3), :, pl.ds(0, 16)], send_sem.at[5, sec, half])
            wait_bytes(qres.at[sec, half, :, :, pl.ds(0, 3 * n_q)], send_sem.at[2, sec, half])
            wait_bytes(pback.at[sec, half, :, :, pl.ds(0, n_q - 2)], send_sem.at[3, sec, half])
            wait_bytes(mate.at[sec, :, :, :, pl.ds(half * LANES, LANES)], mate_send.at[sec, half])
            for at, held in enumerate((out, vgrad)):
                if sec == 0:
                    wait_bytes(held.at[:, :, :, pl.ds(half * LANES, LANES)], out_sem.at[at, half])


def solution(mesh):
    rows, cols = mesh.shape["row"], mesh.shape["col"]

    def local(adjoint_field, velocity, saved_field, gradient_in):
        _, n_p, n_q, length = adjoint_field.shape
        first, second = line_tables(length)
        by_zh = np.arange(length).reshape(4, 4, -1).transpose(1, 0, 2).reshape(4, -1)
        by_zl = np.arange(length).reshape(2, -1)

        def left_table(groups):
            return jnp.asarray(np.concatenate([first[groups], second[groups]], axis=1), jnp.float32)

        right = jnp.asarray(np.concatenate([first.T, second.T], axis=1), jnp.float32)
        field = jax.ShapeDtypeStruct(adjoint_field.shape, jnp.float32)
        q_lines = (2, HALVES, 3, 2, length, LANES)
        p_lines = (2, HALVES, 2, 3, 4, 4, length // 16, LANES)
        q_results = (2, HALVES, 5, 2, length // 2, LANES)
        p_results = (2, HALVES, 2, 5, 2, length // 4, LANES)
        back = (2, HALVES, 5, n_p, n_q, LANES)
        arrays = (
            adjoint_field, velocity, saved_field, gradient_in, left_table(by_zh), left_table(by_zl), right,
        )
        return pl.pallas_call(
            functools.partial(kernel, rows, cols),
            out_shape=(field, field),
            in_specs=[pl.BlockSpec(memory_space=pl.ANY)] * 7,
            out_specs=(pl.BlockSpec(memory_space=pl.ANY),) * 2,
            scratch_shapes=[
                pltpu.VMEM(field.shape, jnp.float32),
                pltpu.VMEM(field.shape, jnp.float32),
                pltpu.SemaphoreType.DMA((2, HALVES)),
                *(pltpu.VMEM(given.shape, given.dtype) for given in arrays),
                pltpu.SemaphoreType.DMA((HALVES + len(arrays) - 1,)),
                pltpu.VMEM((4, length // 2, 3 * length), jnp.bfloat16),
                pltpu.VMEM((2, length, 3 * length), jnp.bfloat16),
                pltpu.VMEM((3 * length, 2 * length), jnp.bfloat16),
                pltpu.VMEM(field.shape, jnp.float32),
                pltpu.VMEM((2, *field.shape), jnp.float32),
                pltpu.VMEM(field.shape, jnp.bfloat16),
                pltpu.VMEM((5, n_p, n_q, length), jnp.float32),
                pltpu.VMEM(q_lines, jnp.float32),
                pltpu.VMEM(p_lines, jnp.float32),
                pltpu.VMEM(q_results, jnp.float32),
                pltpu.VMEM(p_results, jnp.float32),
                pltpu.VMEM(back, jnp.float32),
                pltpu.VMEM(back, jnp.float32),
                pltpu.SemaphoreType.DMA((6, 2, HALVES)),
                pltpu.SemaphoreType.DMA((4, 2, HALVES)),
                pltpu.SemaphoreType.DMA((2, HALVES, 9)),
                pltpu.SemaphoreType.DMA((2, HALVES)),
                pltpu.SemaphoreType.DMA((2, HALVES, 4)),
            ],
            compiler_params=pltpu.CompilerParams(
                collective_id=0, has_side_effects=True, vmem_limit_bytes=60 * 2**20
            ),
        )(*arrays)

    placed = P(None, "col", "row", None)
    return jax.shard_map(
        local,
        mesh=mesh,
        in_specs=(placed, placed, P(None, None, "col", "row", None), placed),
        out_specs=(placed, placed),
        check_vma=False,
    )
```
